32 devices in a mesh: seg: 2 (over y), samp: 4 (over x, core), var: 4 (over z).
Axes of the slice: x: 2, y: 2, z: 4, core: 2. Of those that a mesh axis runs over, the one named last changes fastest.
Arguments:
- dosage: bfloat16 [8192, 4096], P('samp', ('seg', 'var')), parts along dimension 1
- observed: int32 [8, 8192], P(('seg', 'var'), 'samp'), parts along dimension 0, may hold values from 0 to 1, as said below
- band_reach: int32 [8], P(('seg', 'var')), parts along dimension 0, may hold values from 0 to 2
Outputs:
- ld_blocks: float32 [8, 512, 3, 512], P(('seg', 'var'), 'samp'), parts along dimension 0
The draws below stay inside these ranges and needn't reach their ends.
There are 2 independent parts, one for each index of `seg`. The reference program is written for one: setup_inputs(seed, part) draws one part's arguments, and reference() takes and returns one part's arrays. A program takes and returns all parts, laid end to end along the dimension named above; each array names one. Nothing has to cross between parts.
Inputs may be any that keep to these rules, and one draw needn't show every extreme that they name: observed is 0 or 1 for each variant block of each individual; every block is observed for at least one individual.
All inputs are finite; a program needn't handle non-finite values.
Results may differ from the reference program's by a relative error of at most 0.0011.
Values may be sent and summed in bfloat16 or wider, within the bound.
A program may use at most 64 MiB of HBM per device.

```python
import jax
import jax.numpy as jnp
from jax import lax

BLOCK = 512
BAND = 3
SAMPLES = 8192
NBLK = 4
VARIANTS = 2048


def draw_dosage(key, part):
    first_key, second_key = jax.random.split(key, 2)
    noise = jax.random.normal(first_key, (SAMPLES, VARIANTS), jnp.float32)
    mixed = noise + 0.7 * jnp.roll(noise, 1, axis=1) + 0.6 * jnp.roll(noise, BLOCK + 5, axis=1) + 0.5 * jnp.roll(noise, 2 * BLOCK + 37, axis=1)
    frequency = jnp.exp(jax.random.uniform(second_key, (VARIANTS,), jnp.float32, jnp.log(0.05), jnp.log(0.5)))
    logits = jnp.log(frequency / (1.0 - frequency))
    return (2.0 * jax.nn.sigmoid(logits[None, :] + 0.8 * mixed)).astype(jnp.bfloat16)


def disjoint_block(key):
    return jax.random.randint(jax.random.fold_in(key, 11), (), 0, NBLK - 1)


def draw_observed(key, part):
    chosen = disjoint_block(key)
    draws = jax.random.randint(jax.random.fold_in(key, 3), (NBLK, SAMPLES), 0, 1000)
    limit = 300 + 600 * jnp.arange(SAMPLES, dtype=jnp.int32) // SAMPLES
    base = draws < limit[None, :]
    index = jnp.arange(SAMPLES, dtype=jnp.int32)
    blocks = jnp.arange(NBLK, dtype=jnp.int32)
    first_half = index < SAMPLES // 2
    keep_first = jnp.where(blocks[:, None] == chosen, first_half[None, :], True)
    keep_second = jnp.where(blocks[:, None] == chosen + 1, jnp.logical_not(first_half)[None, :], True)
    masked = base & keep_first & keep_second
    forced = jnp.where(blocks[:, None] == chosen + 1, index[None, :] == SAMPLES - 1, index[None, :] == 0)
    return (masked | forced).astype(jnp.int32)


def draw_band_reach(key, part):
    chosen = disjoint_block(key)
    reach = jax.random.randint(jax.random.fold_in(key, 5), (NBLK,), 0, BAND)
    blocks = jnp.arange(NBLK, dtype=jnp.int32)
    return jnp.where(blocks == chosen, BAND - 1, reach).astype(jnp.int32)


def setup_inputs(seed: int = 0, part: int = 0) -> dict:
    streams_of = jax.random.split(jax.random.key(seed), 4)
    part_splits = jax.random.split(jax.random.fold_in(streams_of[3], part), 4)
    dosage = draw_dosage(jax.random.fold_in(jax.random.fold_in(streams_of[3], part), 71), part)
    observed = draw_observed(jax.random.fold_in(jax.random.fold_in(streams_of[3], part), 71), part)
    band_reach = draw_band_reach(jax.random.fold_in(jax.random.fold_in(streams_of[3], part), 71), part)
    return {"dosage": dosage, "observed": observed, "band_reach": band_reach}


EPSILON = 1e-05

def reference(dosage, observed, band_reach):
    blocks = VARIANTS // BLOCK
    weights = observed.astype(jnp.float32)
    values = dosage.astype(jnp.float32).reshape(SAMPLES, blocks, BLOCK)
    totals = lax.optimization_barrier(jnp.sum(weights, axis=1))
    first = jnp.einsum('bs,sbj->bj', weights, values, precision=lax.Precision.HIGHEST)
    second = jnp.einsum('bs,sbj->bj', weights, values * values, precision=lax.Precision.HIGHEST)
    centre = first / totals[:, None]
    spread_inverse = 1.0 / jnp.sqrt(second / totals[:, None] - centre * centre + EPSILON)
    standard = (weights.T[:, :, None] * (values - centre[None]) * spread_inverse[None]).astype(jnp.bfloat16)
    standard_pad = jnp.concatenate([standard, jnp.zeros((SAMPLES, BAND - 1, BLOCK), jnp.bfloat16)], axis=1)
    weights_pad = jnp.concatenate([weights, jnp.zeros((BAND - 1, SAMPLES), jnp.float32)], axis=0)

    def one_block(index):
        own = lax.dynamic_index_in_dim(standard_pad, index, 1, keepdims=False)
        partners = lax.dynamic_slice_in_dim(standard_pad, index, BAND, 1).reshape(SAMPLES, BAND * BLOCK)
        cross = jnp.dot(own.T, partners, preferred_element_type=jnp.float32)
        own_weights = lax.dynamic_index_in_dim(weights_pad, index, 0, keepdims=False)
        band_weights = lax.dynamic_slice_in_dim(weights_pad, index, BAND, 0)
        intersections = jnp.dot(band_weights, own_weights, precision=lax.Precision.HIGHEST)
        keep = jnp.arange(BAND, dtype=jnp.int32) <= lax.dynamic_index_in_dim(band_reach, index, 0, keepdims=False)
        ratio = cross.reshape(BLOCK, BAND, BLOCK) / jnp.maximum(intersections, 1.0)[None, :, None]
        return jnp.where(keep[None, :, None], ratio, jnp.float32(0.0))
    return lax.map(one_block, jnp.arange(blocks, dtype=jnp.int32))
```

```python
import jax
import jax.numpy as jnp
from jax import lax
from jax.sharding import PartitionSpec as P

BAND = 3


EPSILON = 1e-05


def from_behind(shard, axis, by):
    peers = lax.axis_size(axis)
    pairs = [(i, i + by) for i in range(peers) if 0 <= i + by < peers]
    return lax.ppermute(shard, axis, pairs)


def finish_moments(totals, first_sum, second_sum):
    centre = first_sum / totals
    spread_inverse = 1.0 / jnp.sqrt(second_sum / totals - centre * centre + EPSILON)
    return (centre, spread_inverse)


def standardize(values, weights, centre, spread_inverse):
    return (
        weights[:, None] * (values.astype(jnp.float32) - centre[None, :]) * spread_inverse[None, :]
    ).astype(jnp.bfloat16)


def per_device(dosage, observed, band_reach):
    block_width = dosage.shape[1]
    weights = observed[0].astype(jnp.float32)
    weights_half = observed[0].astype(jnp.bfloat16)
    upper_dosage, upper_half = from_behind((dosage, weights_half), "var", -1)
    lower_dosage, lower_half = from_behind((dosage, weights_half), "var", 1)
    first_sum = jnp.dot(weights_half[None, :], dosage, preferred_element_type=jnp.float32)[0]
    second_sum = jnp.sum(weights[:, None] * jnp.square(dosage.astype(jnp.float32)), axis=0)
    own_total = jnp.sum(weights)
    upper_weights = upper_half.astype(jnp.float32)
    lower_weights = lower_half.astype(jnp.float32)
    totals, first_sum, second_sum = lax.psum((own_total, first_sum, second_sum), "samp")
    pairs = lax.psum(
        jnp.stack([own_total, jnp.sum(weights * upper_weights), jnp.sum(lower_weights * upper_weights)]),
        "samp",
    )
    centre, spread_inverse = finish_moments(totals, first_sum, second_sum)
    moments = jnp.stack([centre, spread_inverse])
    upper_moments = from_behind(moments, "var", -1)
    lower_moments = from_behind(moments, "var", 1)
    own = standardize(dosage, weights, centre, spread_inverse)
    upper = standardize(upper_dosage, upper_weights, upper_moments[0], upper_moments[1])
    lower = standardize(lower_dosage, lower_weights, lower_moments[0], lower_moments[1])
    dims = (((0,), (0,)), ((), ()))
    near = lax.dot_general(
        own, jnp.concatenate([own, upper], axis=1), dims, preferred_element_type=jnp.float32
    )
    far = lax.dot_general(lower, upper, dims, preferred_element_type=jnp.float32)
    shared = lax.psum_scatter(
        jnp.concatenate([near, far], axis=1), "samp", scatter_dimension=0, tiled=True
    )
    shared = shared.reshape(1, shared.shape[0], BAND, block_width)
    shared = shared / jnp.maximum(pairs, 1.0)[None, None, :, None]
    far = from_behind(shared[:, :, BAND - 1], "var", -1)
    ratio = jnp.concatenate([shared[:, :, : BAND - 1], far[:, :, None]], axis=2)
    keep = jnp.arange(BAND, dtype=jnp.int32) <= band_reach[0]
    return jnp.where(keep[None, None, :, None], ratio, jnp.float32(0.0))


def solution(mesh):
    return jax.shard_map(
        per_device,
        mesh=mesh,
        in_specs=(P("samp", ("seg", "var")), P(("seg", "var"), "samp"), P(("seg", "var"))),
        out_specs=P(("seg", "var"), "samp", None, None),
        check_vma=False,
    )
```

```python
import functools

import jax
import jax.numpy as jnp
from jax import lax
from jax.experimental import pallas as pl
from jax.experimental.pallas import tpu as pltpu
from jax.sharding import PartitionSpec as P

BAND = 3
EPSILON = 1e-05
LANES = 128
ROWS = 256
CORES = 2
MESH = pl.DeviceIdType.MESH


def remote(src, dst, send, recv, **where):
    return pltpu.make_async_remote_copy(
        src_ref=src, dst_ref=dst, send_sem=send, recv_sem=recv, device_id=where, device_id_type=MESH
    )


def band_kernel(
    peers, depth, dosage, observed, out,
    own, upper, lower, own_t, lower_t, own_w, upper_w, lower_w, upper_flags, lower_flags,
    stats, moments, upper_moments, lower_moments,
    p0, q0, s0, x0, p1, q1, s1, x1, p2, q2, s2, x2, far_out, far_in,
    local_sem, stat_send, stat_recv, flag_sem, moment_sem,
    down_send, down_recv, up_send, up_recv,
    pair_send, pair_recv, cross_send, cross_recv, far_send, far_recv,
):
    samples, width = dosage.shape
    chunks = width // LANES
    rows = width // peers
    chips = peers // CORES
    s = lax.axis_index("samp")
    z = lax.axis_index("var")
    core = lax.rem(s, CORES)
    chip = s // CORES
    sibling = s + 1 - 2 * core
    above = jnp.minimum(z + 1, depth - 1)
    below = jnp.maximum(z - 1, 0)
    sends_down = z >= 1
    sends_up = z <= depth - 3
    has_upper = z <= depth - 2
    has_far = jnp.logical_and(z >= 1, z <= depth - 2)

    def lanes(c):
        return pl.ds(c * LANES, LANES)

    def down(c):
        return remote(dosage.at[:, lanes(c)], upper.at[c], down_send.at[c], down_recv.at[c], var=below)

    def up(c):
        return remote(dosage.at[:, lanes(c)], lower.at[c], up_send.at[c], up_recv.at[c], var=above)

    def flags_down():
        return remote(observed, upper_flags, flag_sem.at[0], flag_sem.at[1], var=below)

    def flags_up():
        return remote(observed, lower_flags, flag_sem.at[2], flag_sem.at[3], var=above)

    def moments_down():
        return remote(moments, upper_moments, moment_sem.at[0], moment_sem.at[1], var=below)

    def moments_up():
        return remote(moments, lower_moments, moment_sem.at[2], moment_sem.at[3], var=above)

    def local(c):
        return pltpu.make_async_copy(dosage.at[:, lanes(c)], own.at[c], local_sem.at[c])

    def start_z(items_down, items_up):
        @pl.when(sends_down)
        def _():
            for item in items_down:
                item().start()

        @pl.when(sends_up)
        def _():
            for item in items_up:
                item().start()

    for c in range(chunks):
        local(c).start()

    barrier = pltpu.get_barrier_semaphore()
    for o in range(1, peers):
        pl.semaphore_signal(
            barrier, inc=1, device_id={"samp": lax.rem(s + o, peers)}, device_id_type=MESH
        )

    @pl.when(z >= 1)
    def _():
        pl.semaphore_signal(barrier, inc=1, device_id={"var": below}, device_id_type=MESH)

    @pl.when(z <= depth - 2)
    def _():
        pl.semaphore_signal(barrier, inc=1, device_id={"var": above}, device_id_type=MESH)

    pl.semaphore_wait(
        barrier, peers - 1 + (z >= 1).astype(jnp.int32) + (z <= depth - 2).astype(jnp.int32)
    )

    early = max(chunks // 2, 1)
    start_z(
        [flags_down] + [functools.partial(down, c) for c in range(early)],
        [flags_up] + [functools.partial(up, c) for c in range(early)],
    )

    def spread_flags(flags, target):
        def body(i, carry):
            at = pl.ds(pl.multiple_of(i * ROWS, ROWS), ROWS)
            row = flags[:, at].astype(jnp.float32)
            target[at, :] = jnp.transpose(jnp.broadcast_to(row, (LANES, ROWS)))
            return carry

        lax.fori_loop(0, samples // ROWS, body, 0)

    spread_flags(observed, own_w)

    for c in range(chunks):
        local(c).wait()

        def body(i, carry, c=c):
            at = pl.ds(pl.multiple_of(i * ROWS, ROWS), ROWS)
            value = own[c, at, :].astype(jnp.float32)
            kept = own_w[at, :] * value
            one = jnp.sum(kept, axis=0, keepdims=True)
            two = jnp.sum(kept * value, axis=0, keepdims=True)
            return (carry[0] + one, carry[1] + two)

        zero = jnp.zeros((1, LANES), jnp.float32)
        one, two = lax.fori_loop(0, samples // ROWS, body, (zero, zero))
        stats[s, 0:1, lanes(c)] = one
        stats[s, 1:2, lanes(c)] = two

    @pl.when(has_upper)
    def _():
        flags_down().wait_recv()

    @pl.when(jnp.logical_not(has_upper))
    def _():
        upper_flags[...] = jnp.zeros_like(upper_flags)

    @pl.when(has_far)
    def _():
        flags_up().wait_recv()

    @pl.when(jnp.logical_not(has_far))
    def _():
        lower_flags[...] = jnp.zeros_like(lower_flags)

    mine = observed[...].astype(jnp.float32)
    uppers = upper_flags[...].astype(jnp.float32)
    lowers = lower_flags[...].astype(jnp.float32)
    for i, product in enumerate((mine, mine * uppers, lowers * uppers)):
        stats[s, 2 + i : 3 + i, :] = jnp.broadcast_to(
            jnp.sum(product, axis=1, keepdims=True), (1, width)
        )
    stats[s, 5:8, :] = jnp.zeros((3, width), jnp.float32)

    def stat(o):
        return remote(
            stats.at[s], stats.at[s], stat_send.at[o], stat_recv.at[o], samp=lax.rem(s + o, peers)
        )

    def stat_in(o):
        return remote(
            stats.at[s],
            stats.at[lax.rem(s + peers - o, peers)],
            stat_send.at[o],
            stat_recv.at[o],
            samp=lax.rem(s + o, peers),
        )

    for o in range(1, peers):
        stat(o).start()
    spread_flags(upper_flags, upper_w)
    spread_flags(lower_flags, lower_w)
    for o in range(1, peers):
        stat_in(o).wait_recv()
    total = stats[0]
    for o in range(1, peers):
        total = total + stats[o]
    count = total[2:3, :]
    centre = total[0:1, :] / count
    inverse = 1.0 / jnp.sqrt(total[1:2, :] / count - centre * centre + EPSILON)
    scales = [1.0 / jnp.maximum(total[2 + k : 3 + k, :], 1.0) for k in range(BAND)]
    moments[0:1, :] = centre
    moments[1:2, :] = inverse
    moments[2:8, :] = jnp.zeros((6, width), jnp.float32)
    start_z(
        [moments_down] + [functools.partial(down, c) for c in range(early, chunks)],
        [moments_up] + [functools.partial(up, c) for c in range(early, chunks)],
    )

    def standardize(block, flags, terms, c, turned):
        centre = terms[0:1, lanes(c)]
        inverse = terms[1:2, lanes(c)]

        def body(i, carry):
            at = pl.ds(pl.multiple_of(i * ROWS, ROWS), ROWS)
            value = block[c, at, :].astype(jnp.float32)
            scaled = flags[at, :] * (value - centre) * inverse
            block[c, at, :] = scaled.astype(jnp.bfloat16)
            if turned is not None:
                turned[lanes(c), at] = jnp.transpose(scaled).astype(jnp.bfloat16)
            return carry

        lax.fori_loop(0, samples // ROWS, body, 0)

    def put(p, first, value, at):
        for j in range(value.shape[0] // rows):
            r = first // rows + j
            p[r % CORES, r // CORES, :, at] = value[j * rows : (j + 1) * rows]

    def dot(a, b):
        return jnp.dot(a, b, preferred_element_type=jnp.float32)

    def pair(unit, r, at, p, q):
        return remote(
            p.at[r % CORES, r // CORES, :, at],
            q.at[r // CORES, :, at],
            pair_send.at[unit, r // CORES],
            pair_recv.at[unit, r // CORES],
            samp=sibling,
        )

    def cross(unit, r, at, sums, x):
        return remote(
            sums.at[r // CORES, :, at],
            x.at[chip, :, at],
            cross_send.at[unit, r // CORES],
            cross_recv.at[unit, chip],
            samp=jnp.int32(r),
        )

    def cross_in(unit, r, g, at, sums, x):
        return remote(
            sums.at[g, :, at],
            x.at[g, :, at],
            cross_send.at[unit, g],
            cross_recv.at[unit, g],
            samp=sibling,
        )

    def owners(spans):
        return [(r, spans(r)) for r in range(peers) if spans(r) is not None]

    def send_pairs(unit, spans, p, q):
        for r, at in owners(spans):

            @pl.when(core != r % CORES)
            def _(r=r, at=at):
                pair(unit, r, at, p, q).start()

    def send_sums(unit, spans, p, q, sums, x):
        for r, at in owners(spans):

            @pl.when(core == r % CORES)
            def _(r=r, at=at):
                pair(unit, r, at, p, q).wait_recv()
                sums[r // CORES, :, at] = p[r % CORES, r // CORES, :, at] + q[r // CORES, :, at]

                @pl.when(chip != r // CORES)
                def _():
                    cross(unit, r, at, sums, x).start()

    def take_sums(unit, spans, sums, x, finish):
        for r, at in owners(spans):

            @pl.when(s == r)
            def _(r=r, at=at):
                value = sums[r // CORES, :, at]
                for g in range(chips):
                    if g != r // CORES:
                        cross_in(unit, r, g, at, sums, x).wait_recv()
                        value = value + x[g, :, at]
                finish(r, at, value)

    def wait_sends(unit, spans, p, q, sums, x):
        for r, at in owners(spans):

            @pl.when(core != r % CORES)
            def _(r=r, at=at):
                pair(unit, r, at, p, q).wait_send()

            @pl.when(jnp.logical_and(core == r % CORES, chip != r // CORES))
            def _(r=r, at=at):
                cross(unit, r, at, sums, x).wait_send()

    whole = pl.ds(0, width)

    def store_at(k, offset):
        def finish(r, at, value):
            out[k, :, pl.ds(at.start + offset, at.size)] = value * scales[k][:, : at.size]

        return finish

    for c in range(chunks):
        standardize(own, own_w, moments, c, own_t)
    for c in range(chunks):
        put(p0, 0, dot(own_t[...], own[c]), lanes(c))
    send_pairs(0, lambda r: whole, p0, q0)
    send_sums(0, lambda r: whole, p0, q0, s0, x0)

    @pl.when(has_upper)
    def _():
        moments_down().wait_recv()

    @pl.when(has_far)
    def _():
        moments_up().wait_recv()

    take_sums(0, lambda r: whole, s0, x0, store_at(0, 0))

    strip = pl.ds(0, LANES)

    def far_spans(c):
        def spans(r):
            q = r * rows // LANES
            if q < c:
                return lanes(c)
            if q == c:
                return pl.ds(0, (c + 1) * LANES)
            return None

        return spans

    def ship(c, at):
        return remote(
            far_out.at[:, at], far_in.at[:, at], far_send.at[c], far_recv.at[c], var=below
        )

    for c in range(chunks):
        near, far = 1 + c, 1 + chunks + c
        near_refs = (p1.at[c], q1.at[c], s1.at[c], x1.at[c])
        far_refs = (p2, q2, s2, x2)

        @pl.when(has_upper)
        def _(c=c, near=near, near_refs=near_refs):
            down(c).wait_recv()
            standardize(upper, upper_w, upper_moments, c, None)
            put(near_refs[0], 0, dot(own_t[...], upper[c]), strip)
            send_pairs(near, lambda r: strip, *near_refs[:2])

        @pl.when(has_far)
        def _(c=c, far=far):
            up(c).wait_recv()
            standardize(lower, lower_w, lower_moments, c, lower_t)
            for j in range(c + 1):
                put(p2, c * LANES, dot(lower_t[lanes(c), :], upper[j]), lanes(j))
            if c:
                put(p2, 0, dot(lower_t[: c * LANES, :], upper[c]), lanes(c))
            send_pairs(far, far_spans(c), *far_refs[:2])

        @pl.when(has_upper)
        def _(c=c, near=near, near_refs=near_refs):
            send_sums(near, lambda r: strip, *near_refs)

        @pl.when(has_far)
        def _(c=c, far=far):
            send_sums(far, far_spans(c), *far_refs)

            def finish(r, at, value):
                far_out[:, at] = value * scales[2][:, : at.size]
                ship(c, at).start()

            take_sums(far, far_spans(c), s2, x2, finish)

        @pl.when(has_upper)
        def _(c=c, near=near, near_refs=near_refs):
            take_sums(near, lambda r: strip, *near_refs[2:], store_at(1, c * LANES))

    @pl.when(jnp.logical_not(has_upper))
    def _():
        out[1] = jnp.zeros((rows, width), jnp.float32)

    for c in range(chunks):
        for r, at in owners(far_spans(c)):

            @pl.when(jnp.logical_and(sends_up, s == r))
            def _(c=c, at=at):
                ship(c, at).wait_recv()

    @pl.when(sends_up)
    def _():
        out[2] = far_in[...]

    @pl.when(jnp.logical_not(sends_up))
    def _():
        out[2] = jnp.zeros((rows, width), jnp.float32)

    for o in range(1, peers):
        stat(o).wait_send()

    @pl.when(sends_down)
    def _():
        flags_down().wait_send()
        moments_down().wait_send()
        for c in range(chunks):
            down(c).wait_send()

    @pl.when(sends_up)
    def _():
        flags_up().wait_send()
        moments_up().wait_send()
        for c in range(chunks):
            up(c).wait_send()

    wait_sends(0, lambda r: whole, p0, q0, s0, x0)

    @pl.when(has_upper)
    def _():
        for c in range(chunks):
            wait_sends(1 + c, lambda r: strip, p1.at[c], q1.at[c], s1.at[c], x1.at[c])

    @pl.when(has_far)
    def _():
        for c in range(chunks):
            wait_sends(1 + chunks + c, far_spans(c), p2, q2, s2, x2)
            for r, at in owners(far_spans(c)):

                @pl.when(s == r)
                def _(c=c, at=at):
                    ship(c, at).wait_send()


def per_device(peers, depth, dosage, observed, band_reach):
    samples, width = dosage.shape
    chunks = width // LANES
    rows = width // peers
    chips = peers // CORES
    half, full = jnp.bfloat16, jnp.float32
    dma = pltpu.SemaphoreType.DMA
    units = 1 + 2 * chunks
    block = pltpu.VMEM((chunks, samples, LANES), half)
    turned = pltpu.VMEM((width, samples), half)
    column = pltpu.VMEM((samples, LANES), full)
    flags = pltpu.VMEM((1, samples), jnp.int32)
    terms = pltpu.VMEM((8, width), full)
    wide = [pltpu.VMEM((CORES, chips, rows, width), full)] + [
        pltpu.VMEM((chips, rows, width), full)
    ] * 3
    strips = [pltpu.VMEM((chunks, CORES, chips, rows, LANES), full)] + [
        pltpu.VMEM((chunks, chips, rows, LANES), full)
    ] * 3
    result = pltpu.VMEM((rows, width), full)
    values = pl.pallas_call(
        functools.partial(band_kernel, peers, depth),
        out_shape=jax.ShapeDtypeStruct((BAND, rows, width), full),
        in_specs=[pl.BlockSpec(memory_space=pl.ANY), pl.BlockSpec(memory_space=pltpu.VMEM)],
        out_specs=pl.BlockSpec(memory_space=pltpu.VMEM),
        scratch_shapes=[block] * 3
        + [turned] * 2
        + [column] * 3
        + [flags] * 2
        + [pltpu.VMEM((peers, 8, width), full)]
        + [terms] * 3
        + wide
        + strips
        + wide
        + [result] * 2
        + [dma((chunks,)), dma((peers,)), dma((peers,)), dma((4,)), dma((4,))]
        + [dma((chunks,))] * 4
        + [dma((units, chips))] * 4
        + [dma((chunks,))] * 2,
        compiler_params=pltpu.CompilerParams(
            collective_id=0, has_side_effects=True, vmem_limit_bytes=52 * 1024 * 1024
        ),
        cost_estimate=pl.CostEstimate(
            flops=2 * BAND * width * width * samples,
            bytes_accessed=2 * samples * width,
            transcendentals=0,
        ),
    )(dosage, observed)
    keep = jnp.arange(BAND, dtype=jnp.int32) <= band_reach[0]
    return jnp.where(
        keep[None, None, :, None], jnp.transpose(values, (1, 0, 2))[None], jnp.float32(0.0)
    )


def solution(mesh):
    return jax.shard_map(
        functools.partial(per_device, mesh.shape["samp"], mesh.shape["var"]),
        mesh=mesh,
        in_specs=(P("samp", ("seg", "var")), P(("seg", "var"), "samp"), P(("seg", "var"))),
        out_specs=P(("seg", "var"), "samp", None, None),
        check_vma=False,
    )
```

```python
import functools

import jax
import jax.numpy as jnp
from jax import lax
from jax.experimental import pallas as pl
from jax.experimental.pallas import tpu as pltpu
from jax.sharding import PartitionSpec as P

BAND = 3
EPSILON = 1e-05
LANES = 128
ROWS = 256
CORES = 2
MESH = pl.DeviceIdType.MESH


def pieces_of(samples, chunks, c):
    if c < chunks - 1 or samples % (8 * ROWS):
        return [(0, samples)]
    part = samples // 8
    return [(0, 4 * part), (4 * part, 2 * part), (6 * part, part), (7 * part, part)]


def remote(src, dst, send, recv, **where):
    return pltpu.make_async_remote_copy(
        src_ref=src, dst_ref=dst, send_sem=send, recv_sem=recv, device_id=where, device_id_type=MESH
    )


def band_kernel(
    peers, depth, dosage, observed, out,
    own, upper, lower, own_t, lower_t, own_w, upper_w, lower_w, flags, upper_flags, lower_flags,
    stats, moments, upper_moments, lower_moments,
    p0, q0, s0, x0, p1, q1, s1, x1, p2, q2, s2, x2, far_out, far_in,
    local_sem, stat_send, stat_recv, flag_sem, moment_sem,
    down_send, down_recv, up_send, up_recv,
    pair_send, pair_recv, cross_send, cross_recv, far_send, far_recv,
):
    samples, width = dosage.shape
    chunks = width // LANES
    rows = width // peers
    chips = peers // CORES
    s = lax.axis_index("samp")
    z = lax.axis_index("var")
    core = lax.rem(s, CORES)
    chip = s // CORES
    sibling = s + 1 - 2 * core
    above = jnp.minimum(z + 1, depth - 1)
    below = jnp.maximum(z - 1, 0)
    sends_down = z >= 1
    sends_up = z <= depth - 3
    has_upper = z <= depth - 2
    has_far = jnp.logical_and(z >= 1, z <= depth - 2)

    def lanes(c):
        return pl.ds(c * LANES, LANES)

    def slot(c, i):
        return sum(len(pieces_of(samples, chunks, b)) for b in range(c)) + i

    def down(c, i):
        first, size = pieces_of(samples, chunks, c)[i]
        at, k = pl.ds(first, size), slot(c, i)
        return remote(
            dosage.at[at, lanes(c)], upper.at[c, at, :], down_send.at[k], down_recv.at[k], var=below
        )

    def up(c, i):
        first, size = pieces_of(samples, chunks, c)[i]
        at, k = pl.ds(first, size), slot(c, i)
        return remote(
            dosage.at[at, lanes(c)], lower.at[c, at, :], up_send.at[k], up_recv.at[k], var=above
        )

    def bulk(copy, cs):
        return [
            functools.partial(copy, c, i)
            for c in cs
            for i in range(len(pieces_of(samples, chunks, c)))
        ]

    def flags_down():
        return remote(observed, upper_flags, flag_sem.at[0], flag_sem.at[1], var=below)

    def flags_up():
        return remote(observed, lower_flags, flag_sem.at[2], flag_sem.at[3], var=above)

    def moments_down():
        return remote(moments, upper_moments, moment_sem.at[0], moment_sem.at[1], var=below)

    def moments_up():
        return remote(moments, lower_moments, moment_sem.at[2], moment_sem.at[3], var=above)

    def local(c):
        return pltpu.make_async_copy(dosage.at[:, lanes(c)], own.at[c], local_sem.at[c])

    def start_z(items_down, items_up):
        @pl.when(sends_down)
        def _():
            for item in items_down:
                item().start()

        @pl.when(sends_up)
        def _():
            for item in items_up:
                item().start()

    for c in range(chunks):
        local(c).start()
    fetch = pltpu.make_async_copy(observed, flags, local_sem.at[chunks])
    fetch.start()

    barrier = pltpu.get_barrier_semaphore()
    for o in range(1, peers):
        pl.semaphore_signal(
            barrier, inc=1, device_id={"samp": lax.rem(s + o, peers)}, device_id_type=MESH
        )

    @pl.when(z >= 1)
    def _():
        pl.semaphore_signal(barrier, inc=1, device_id={"var": below}, device_id_type=MESH)

    @pl.when(z <= depth - 2)
    def _():
        pl.semaphore_signal(barrier, inc=1, device_id={"var": above}, device_id_type=MESH)

    pl.semaphore_wait(
        barrier, peers - 1 + (z >= 1).astype(jnp.int32) + (z <= depth - 2).astype(jnp.int32)
    )

    early = max(chunks // 2, 1)
    start_z(
        [flags_down] + bulk(down, range(early)),
        [flags_up] + bulk(up, range(early)),
    )

    def spread_flags(flags, target):
        def body(i, carry):
            at = pl.ds(pl.multiple_of(i * ROWS, ROWS), ROWS)
            row = flags[:, at].astype(jnp.float32)
            target[at, :] = jnp.transpose(jnp.broadcast_to(row, (LANES, ROWS)))
            return carry

        lax.fori_loop(0, samples // ROWS, body, 0)

    fetch.wait()
    spread_flags(flags, own_w)

    for c in range(chunks):
        local(c).wait()

        def body(i, carry, c=c):
            at = pl.ds(pl.multiple_of(i * ROWS, ROWS), ROWS)
            value = own[c, at, :].astype(jnp.float32)
            kept = own_w[at, :] * value
            one = jnp.sum(kept, axis=0, keepdims=True)
            two = jnp.sum(kept * value, axis=0, keepdims=True)
            return (carry[0] + one, carry[1] + two)

        zero = jnp.zeros((1, LANES), jnp.float32)
        one, two = lax.fori_loop(0, samples // ROWS, body, (zero, zero))
        stats[s, 0:1, lanes(c)] = one
        stats[s, 1:2, lanes(c)] = two

    @pl.when(has_upper)
    def _():
        flags_down().wait_recv()

    @pl.when(jnp.logical_not(has_upper))
    def _():
        upper_flags[...] = jnp.zeros_like(upper_flags)

    @pl.when(has_far)
    def _():
        flags_up().wait_recv()

    @pl.when(jnp.logical_not(has_far))
    def _():
        lower_flags[...] = jnp.zeros_like(lower_flags)

    mine = flags[...].astype(jnp.float32)
    uppers = upper_flags[...].astype(jnp.float32)
    lowers = lower_flags[...].astype(jnp.float32)
    for i, product in enumerate((mine, mine * uppers, lowers * uppers)):
        stats[s, 2 + i : 3 + i, :] = jnp.broadcast_to(
            jnp.sum(product, axis=1, keepdims=True), (1, width)
        )
    stats[s, 5:8, :] = jnp.zeros((3, width), jnp.float32)

    def stat(o):
        return remote(
            stats.at[s], stats.at[s], stat_send.at[o], stat_recv.at[o], samp=lax.rem(s + o, peers)
        )

    def stat_in(o):
        return remote(
            stats.at[s],
            stats.at[lax.rem(s + peers - o, peers)],
            stat_send.at[o],
            stat_recv.at[o],
            samp=lax.rem(s + o, peers),
        )

    for o in range(1, peers):
        stat(o).start()
    spread_flags(upper_flags, upper_w)
    spread_flags(lower_flags, lower_w)
    for o in range(1, peers):
        stat_in(o).wait_recv()
    total = stats[0]
    for o in range(1, peers):
        total = total + stats[o]
    count = total[2:3, :]
    centre = total[0:1, :] / count
    inverse = 1.0 / jnp.sqrt(total[1:2, :] / count - centre * centre + EPSILON)
    scales = [1.0 / jnp.maximum(total[2 + k : 3 + k, :], 1.0) for k in range(BAND)]
    moments[0:1, :] = centre
    moments[1:2, :] = inverse
    moments[2:8, :] = jnp.zeros((6, width), jnp.float32)
    start_z(
        [moments_down] + bulk(down, range(early, chunks)),
        [moments_up] + bulk(up, range(early, chunks)),
    )

    def standardize(block, kept, terms, c, turned, span=(0, samples)):
        centre = terms[0:1, lanes(c)]
        inverse = terms[1:2, lanes(c)]

        def body(i, carry):
            at = pl.ds(pl.multiple_of(i * ROWS, ROWS), ROWS)
            value = block[c, at, :].astype(jnp.float32)
            scaled = kept[at, :] * (value - centre) * inverse
            block[c, at, :] = scaled.astype(jnp.bfloat16)
            if turned is not None:
                turned[lanes(c), at] = jnp.transpose(scaled).astype(jnp.bfloat16)
            return carry

        lax.fori_loop(span[0] // ROWS, (span[0] + span[1]) // ROWS, body, 0)

    def put(p, first, value, at, add=False):
        for j in range(value.shape[0] // rows):
            r = first // rows + j
            term = value[j * rows : (j + 1) * rows]
            if add:
                term = term + p[r % CORES, r // CORES, :, at]
            p[r % CORES, r // CORES, :, at] = term

    def dot(a, b):
        return jnp.dot(a, b, preferred_element_type=jnp.float32)

    def pair(unit, r, k, at, p, q):
        return remote(
            p.at[r % CORES, r // CORES, :, at],
            q.at[r // CORES, :, at],
            pair_send.at[unit, r // CORES, k],
            pair_recv.at[unit, r // CORES, k],
            samp=sibling,
        )

    def cross(unit, r, k, at, sums, x):
        return remote(
            sums.at[r // CORES, :, at],
            x.at[chip, :, at],
            cross_send.at[unit, r // CORES, k],
            cross_recv.at[unit, chip, k],
            samp=jnp.int32(r),
        )

    def cross_in(unit, r, g, k, at, sums, x):
        return remote(
            sums.at[g, :, at],
            x.at[g, :, at],
            cross_send.at[unit, g, k],
            cross_recv.at[unit, g, k],
            samp=sibling,
        )

    def owners(spans):
        return [(r, k, at) for r in range(peers) for k, at in enumerate(spans(r))]

    def send_pairs(unit, spans, p, q):
        for r, k, at in owners(spans):

            @pl.when(core != r % CORES)
            def _(r=r, k=k, at=at):
                pair(unit, r, k, at, p, q).start()

    def send_sums(unit, spans, p, q, sums, x):
        for r, k, at in owners(spans):

            @pl.when(core == r % CORES)
            def _(r=r, k=k, at=at):
                pair(unit, r, k, at, p, q).wait_recv()
                sums[r // CORES, :, at] = p[r % CORES, r // CORES, :, at] + q[r // CORES, :, at]

                @pl.when(chip != r // CORES)
                def _():
                    cross(unit, r, k, at, sums, x).start()

    def take_sums(unit, spans, sums, x, finish):
        for r, k, at in owners(spans):

            @pl.when(s == r)
            def _(r=r, k=k, at=at):
                value = sums[r // CORES, :, at]
                for g in range(chips):
                    if g != r // CORES:
                        cross_in(unit, r, g, k, at, sums, x).wait_recv()
                        value = value + x[g, :, at]
                finish(r, k, at, value)

    def wait_sends(unit, spans, p, q, sums, x):
        for r, k, at in owners(spans):

            @pl.when(core != r % CORES)
            def _(r=r, k=k, at=at):
                pair(unit, r, k, at, p, q).wait_send()

            @pl.when(jnp.logical_and(core == r % CORES, chip != r // CORES))
            def _(r=r, k=k, at=at):
                cross(unit, r, k, at, sums, x).wait_send()

    whole = pl.ds(0, width)

    def store_at(band, offset):
        def finish(r, k, at, value):
            out[band, :, pl.ds(at.start + offset, at.size)] = value * scales[band][:, : at.size]

        return finish

    for c in range(chunks):
        standardize(own, own_w, moments, c, own_t)
    for c in range(chunks):
        put(p0, 0, dot(own_t[...], own[c]), lanes(c))
    send_pairs(0, lambda r: [whole], p0, q0)
    send_sums(0, lambda r: [whole], p0, q0, s0, x0)

    @pl.when(has_upper)
    def _():
        moments_down().wait_recv()

    @pl.when(has_far)
    def _():
        moments_up().wait_recv()

    take_sums(0, lambda r: [whole], s0, x0, store_at(0, 0))

    strip = pl.ds(0, LANES)

    def far_spans(c):
        def spans(r):
            q = r * rows // LANES
            if q < c:
                return [lanes(c)]
            if q == c < chunks - 1:
                return [pl.ds(0, (c + 1) * LANES)]
            if q == c:
                return [lanes(j) for j in range(chunks)]
            return []

        return spans

    def ship(c, k, at):
        return remote(
            far_out.at[:, at], far_in.at[:, at], far_send.at[c, k], far_recv.at[c, k], var=below
        )

    for c in range(chunks):
        near, far = 1 + c, 1 + chunks + c
        near_refs = (p1.at[c], q1.at[c], s1.at[c], x1.at[c])
        far_refs = (p2, q2, s2, x2)

        for i, (first, size) in enumerate(pieces_of(samples, chunks, c)):
            at, add = pl.ds(first, size), i > 0

            @pl.when(has_upper)
            def _(c=c, i=i, first=first, size=size):
                down(c, i).wait_recv()
                standardize(upper, upper_w, upper_moments, c, None, (first, size))

            @pl.when(has_far)
            def _(c=c, i=i, at=at, add=add, first=first, size=size):
                up(c, i).wait_recv()
                standardize(lower, lower_w, lower_moments, c, lower_t, (first, size))
                for j in range(c + 1):
                    put(p2, c * LANES, dot(lower_t[lanes(c), at], upper[j, at, :]), lanes(j), add)
                if c:
                    put(p2, 0, dot(lower_t[: c * LANES, at], upper[c, at, :]), lanes(c), add)

            if first + size == samples:

                @pl.when(has_far)
                def _(c=c, far=far):
                    send_pairs(far, far_spans(c), p2, q2)

            @pl.when(has_upper)
            def _(c=c, at=at, add=add):
                put(p1.at[c], 0, dot(own_t[:, at], upper[c, at, :]), strip, add)

        @pl.when(has_upper)
        def _(c=c, near=near):
            send_pairs(near, lambda r: [strip], p1.at[c], q1.at[c])

        @pl.when(has_far)
        def _(c=c, far=far):
            send_sums(far, far_spans(c), *far_refs)

        @pl.when(has_upper)
        def _(c=c, near=near, near_refs=near_refs):
            send_sums(near, lambda r: [strip], *near_refs)

        if c == chunks - 1:
            for b in range(chunks - 1):
                for r, k, at in owners(far_spans(b)):

                    @pl.when(jnp.logical_and(jnp.logical_and(has_far, z >= 2), s == r))
                    def _(b=b, k=k, at=at):
                        ship(b, k, at).start()

        @pl.when(has_far)
        def _(c=c, far=far):
            def finish(r, k, at, value):
                far_out[:, at] = value * scales[2][:, : at.size]
                if c == chunks - 1:
                    ship(c, k, at).start()
                else:

                    @pl.when(z == 1)
                    def _():
                        ship(c, k, at).start()

            take_sums(far, far_spans(c), s2, x2, finish)

        @pl.when(has_upper)
        def _(c=c, near=near, near_refs=near_refs):
            take_sums(near, lambda r: [strip], *near_refs[2:], store_at(1, c * LANES))

    @pl.when(jnp.logical_not(has_upper))
    def _():
        out[1] = jnp.zeros((rows, width), jnp.float32)

    for c in range(chunks):
        for r, k, at in owners(far_spans(c)):

            @pl.when(jnp.logical_and(sends_up, s == r))
            def _(c=c, k=k, at=at):
                ship(c, k, at).wait_recv()

    @pl.when(sends_up)
    def _():
        out[2] = far_in[...]

    @pl.when(jnp.logical_not(sends_up))
    def _():
        out[2] = jnp.zeros((rows, width), jnp.float32)

    for o in range(1, peers):
        stat(o).wait_send()

    @pl.when(sends_down)
    def _():
        flags_down().wait_send()
        moments_down().wait_send()
        for item in bulk(down, range(chunks)):
            item().wait_send()

    @pl.when(sends_up)
    def _():
        flags_up().wait_send()
        moments_up().wait_send()
        for item in bulk(up, range(chunks)):
            item().wait_send()

    wait_sends(0, lambda r: [whole], p0, q0, s0, x0)

    @pl.when(has_upper)
    def _():
        for c in range(chunks):
            wait_sends(1 + c, lambda r: [strip], p1.at[c], q1.at[c], s1.at[c], x1.at[c])

    @pl.when(has_far)
    def _():
        for c in range(chunks):
            wait_sends(1 + chunks + c, far_spans(c), p2, q2, s2, x2)
            for r, k, at in owners(far_spans(c)):

                @pl.when(s == r)
                def _(c=c, k=k, at=at):
                    ship(c, k, at).wait_send()


def per_device(peers, depth, dosage, observed, band_reach):
    samples, width = dosage.shape
    chunks = width // LANES
    rows = width // peers
    chips = peers // CORES
    half, full = jnp.bfloat16, jnp.float32
    dma = pltpu.SemaphoreType.DMA
    units = 1 + 2 * chunks
    block = pltpu.VMEM((chunks, samples, LANES), half)
    turned = pltpu.VMEM((width, samples), half)
    column = pltpu.VMEM((samples, LANES), full)
    flags = pltpu.VMEM((1, samples), jnp.int32)
    terms = pltpu.VMEM((8, width), full)
    wide = [pltpu.VMEM((CORES, chips, rows, width), full)] + [
        pltpu.VMEM((chips, rows, width), full)
    ] * 3
    strips = [pltpu.VMEM((chunks, CORES, chips, rows, LANES), full)] + [
        pltpu.VMEM((chunks, chips, rows, LANES), full)
    ] * 3
    result = pltpu.VMEM((rows, width), full)
    values = pl.pallas_call(
        functools.partial(band_kernel, peers, depth),
        out_shape=jax.ShapeDtypeStruct((BAND, rows, width), full),
        in_specs=[pl.BlockSpec(memory_space=pl.ANY)] * 2,
        out_specs=pl.BlockSpec(memory_space=pltpu.VMEM),
        scratch_shapes=[block] * 3
        + [turned] * 2
        + [column] * 3
        + [flags] * 3
        + [pltpu.VMEM((peers, 8, width), full)]
        + [terms] * 3
        + wide
        + strips
        + wide
        + [result] * 2
        + [dma((chunks + 1,)), dma((peers,)), dma((peers,)), dma((4,)), dma((4,))]
        + [dma((sum(len(pieces_of(samples, chunks, c)) for c in range(chunks)),))] * 4
        + [dma((units, chips, chunks))] * 4
        + [dma((chunks, chunks))] * 2,
        compiler_params=pltpu.CompilerParams(
            collective_id=0, has_side_effects=True, vmem_limit_bytes=52 * 1024 * 1024
        ),
        cost_estimate=pl.CostEstimate(
            flops=2 * BAND * width * width * samples,
            bytes_accessed=2 * samples * width,
            transcendentals=0,
        ),
    )(dosage, observed)
    keep = jnp.arange(BAND, dtype=jnp.int32) <= band_reach[0]
    return jnp.where(
        keep[None, None, :, None], jnp.transpose(values, (1, 0, 2))[None], jnp.float32(0.0)
    )


def solution(mesh):
    return jax.shard_map(
        functools.partial(per_device, mesh.shape["samp"], mesh.shape["var"]),
        mesh=mesh,
        in_specs=(P("samp", ("seg", "var")), P(("seg", "var"), "samp"), P(("seg", "var"))),
        out_specs=P(("seg", "var"), "samp", None, None),
        check_vma=False,
    )
```

```python
import functools

import jax
import jax.numpy as jnp
from jax import lax
from jax.experimental import pallas as pl
from jax.experimental.pallas import tpu as pltpu
from jax.sharding import PartitionSpec as P

BAND = 3
EPSILON = 1e-05
LANES = 128
ROWS = 256
CORES = 2
MESH = pl.DeviceIdType.MESH


def pieces_of(samples, chunks, c):
    if c < chunks - 1 or samples % (8 * ROWS):
        return [(0, samples)]
    part = samples // 8
    return [(0, 4 * part), (4 * part, 2 * part), (6 * part, part), (7 * part, part)]


def remote(src, dst, send, recv, **where):
    return pltpu.make_async_remote_copy(
        src_ref=src, dst_ref=dst, send_sem=send, recv_sem=recv, device_id=where, device_id_type=MESH
    )


def band_kernel(
    peers, depth, dosage, observed, out,
    own, upper, lower, own_t, lower_t, own_w, upper_w, lower_w, flags, upper_flags, lower_flags,
    stats, moments, upper_moments, lower_moments,
    p0, q0, s0, x0, p1, q1, s1, x1, p2, q2, s2, x2, far_out, far_in,
    local_sem, stat_send, stat_recv, flag_sem, moment_sem,
    down_send, down_recv, up_send, up_recv,
    pair_send, pair_recv, cross_send, cross_recv, far_send, far_recv,
):
    samples, width = dosage.shape
    chunks = width // LANES
    rows = width // peers
    chips = peers // CORES
    s = lax.axis_index("samp")
    z = lax.axis_index("var")
    core = lax.rem(s, CORES)
    chip = s // CORES
    sibling = s + 1 - 2 * core
    above = jnp.minimum(z + 1, depth - 1)
    below = jnp.maximum(z - 1, 0)
    sends_down = z >= 1
    sends_up = z <= depth - 3
    has_upper = z <= depth - 2
    has_far = jnp.logical_and(z >= 1, z <= depth - 2)

    def lanes(c):
        return pl.ds(c * LANES, LANES)

    def slot(c, i):
        return sum(len(pieces_of(samples, chunks, b)) for b in range(c)) + i

    def down(c, i):
        first, size = pieces_of(samples, chunks, c)[i]
        at, k = pl.ds(first, size), slot(c, i)
        return remote(
            dosage.at[at, lanes(c)], upper.at[c, at, :], down_send.at[k], down_recv.at[k], var=below
        )

    def up(c, i):
        first, size = pieces_of(samples, chunks, c)[i]
        at, k = pl.ds(first, size), slot(c, i)
        return remote(
            dosage.at[at, lanes(c)], lower.at[c, at, :], up_send.at[k], up_recv.at[k], var=above
        )

    def bulk(copy, cs):
        return [
            functools.partial(copy, c, i)
            for c in cs
            for i in range(len(pieces_of(samples, chunks, c)))
        ]

    def flags_down():
        return remote(observed, upper_flags, flag_sem.at[0], flag_sem.at[1], var=below)

    def flags_up():
        return remote(observed, lower_flags, flag_sem.at[2], flag_sem.at[3], var=above)

    def moments_down():
        return remote(moments, upper_moments, moment_sem.at[0], moment_sem.at[1], var=below)

    def moments_up():
        return remote(moments, lower_moments, moment_sem.at[2], moment_sem.at[3], var=above)

    def local(c):
        return pltpu.make_async_copy(dosage.at[:, lanes(c)], own.at[c], local_sem.at[c])

    def start_z(items_down, items_up):
        @pl.when(sends_down)
        def _():
            for item in items_down:
                item().start()

        @pl.when(sends_up)
        def _():
            for item in items_up:
                item().start()

    for c in range(chunks):
        local(c).start()
    fetch = pltpu.make_async_copy(observed, flags, local_sem.at[chunks])
    fetch.start()

    barrier = pltpu.get_barrier_semaphore()
    for o in range(1, peers):
        pl.semaphore_signal(
            barrier, inc=1, device_id={"samp": lax.rem(s + o, peers)}, device_id_type=MESH
        )

    @pl.when(z >= 1)
    def _():
        pl.semaphore_signal(barrier, inc=1, device_id={"var": below}, device_id_type=MESH)

    @pl.when(z <= depth - 2)
    def _():
        pl.semaphore_signal(barrier, inc=1, device_id={"var": above}, device_id_type=MESH)

    pl.semaphore_wait(
        barrier, peers - 1 + (z >= 1).astype(jnp.int32) + (z <= depth - 2).astype(jnp.int32)
    )

    early = 1
    start_z(
        [flags_down] + bulk(down, range(early)),
        [flags_up] + bulk(up, range(early)),
    )

    def spread_flags(flags, target):
        def body(i, carry):
            at = pl.ds(pl.multiple_of(i * ROWS, ROWS), ROWS)
            row = flags[:, at].astype(jnp.float32)
            target[at, :] = jnp.transpose(jnp.broadcast_to(row, (LANES, ROWS)))
            return carry

        lax.fori_loop(0, samples // ROWS, body, 0)

    fetch.wait()
    spread_flags(flags, own_w)

    for c in range(chunks):
        local(c).wait()

        def body(i, carry, c=c):
            at = pl.ds(pl.multiple_of(i * ROWS, ROWS), ROWS)
            value = own[c, at, :].astype(jnp.float32)
            kept = own_w[at, :] * value
            one = jnp.sum(kept, axis=0, keepdims=True)
            two = jnp.sum(kept * value, axis=0, keepdims=True)
            return (carry[0] + one, carry[1] + two)

        zero = jnp.zeros((1, LANES), jnp.float32)
        one, two = lax.fori_loop(0, samples // ROWS, body, (zero, zero))
        stats[s, 0:1, lanes(c)] = one
        stats[s, 1:2, lanes(c)] = two

    @pl.when(has_upper)
    def _():
        flags_down().wait_recv()

    @pl.when(jnp.logical_not(has_upper))
    def _():
        upper_flags[...] = jnp.zeros_like(upper_flags)

    @pl.when(has_far)
    def _():
        flags_up().wait_recv()

    @pl.when(jnp.logical_not(has_far))
    def _():
        lower_flags[...] = jnp.zeros_like(lower_flags)

    mine = flags[...].astype(jnp.float32)
    uppers = upper_flags[...].astype(jnp.float32)
    lowers = lower_flags[...].astype(jnp.float32)
    for i, product in enumerate((mine, mine * uppers, lowers * uppers)):
        stats[s, 2 + i : 3 + i, :] = jnp.broadcast_to(
            jnp.sum(product, axis=1, keepdims=True), (1, width)
        )
    stats[s, 5:8, :] = jnp.zeros((3, width), jnp.float32)

    def stat(o):
        return remote(
            stats.at[s], stats.at[s], stat_send.at[o], stat_recv.at[o], samp=lax.rem(s + o, peers)
        )

    def stat_in(o):
        return remote(
            stats.at[s],
            stats.at[lax.rem(s + peers - o, peers)],
            stat_send.at[o],
            stat_recv.at[o],
            samp=lax.rem(s + o, peers),
        )

    for o in range(1, peers):
        stat(o).start()
    spread_flags(upper_flags, upper_w)
    spread_flags(lower_flags, lower_w)
    for o in range(1, peers):
        stat_in(o).wait_recv()
    total = stats[0]
    for o in range(1, peers):
        total = total + stats[o]
    count = total[2:3, :]
    centre = total[0:1, :] / count
    inverse = 1.0 / jnp.sqrt(total[1:2, :] / count - centre * centre + EPSILON)
    scales = [1.0 / jnp.maximum(total[2 + k : 3 + k, :], 1.0) for k in range(BAND)]
    moments[0:1, :] = centre
    moments[1:2, :] = inverse
    moments[2:8, :] = jnp.zeros((6, width), jnp.float32)
    start_z(
        [moments_down] + bulk(down, range(early, chunks)),
        [moments_up] + bulk(up, range(early, chunks)),
    )

    def standardize(block, kept, terms, c, turned, span=(0, samples)):
        centre = terms[0:1, lanes(c)]
        inverse = terms[1:2, lanes(c)]

        def body(i, carry):
            at = pl.ds(pl.multiple_of(i * ROWS, ROWS), ROWS)
            value = block[c, at, :].astype(jnp.float32)
            scaled = kept[at, :] * (value - centre) * inverse
            block[c, at, :] = scaled.astype(jnp.bfloat16)
            if turned is not None:
                turned[lanes(c), at] = jnp.transpose(scaled).astype(jnp.bfloat16)
            return carry

        lax.fori_loop(span[0] // ROWS, (span[0] + span[1]) // ROWS, body, 0)

    def put(p, first, value, at, add=False):
        for j in range(value.shape[0] // rows):
            r = first // rows + j
            term = value[j * rows : (j + 1) * rows]
            if add:
                term = term + p[r % CORES, r // CORES, :, at]
            p[r % CORES, r // CORES, :, at] = term

    def dot(a, b):
        return jnp.dot(a, b, preferred_element_type=jnp.float32)

    def pair(unit, r, k, at, p, q):
        return remote(
            p.at[r % CORES, r // CORES, :, at],
            q.at[r // CORES, :, at],
            pair_send.at[unit, r // CORES, k],
            pair_recv.at[unit, r // CORES, k],
            samp=sibling,
        )

    def cross(unit, r, k, at, sums, x):
        return remote(
            sums.at[r // CORES, :, at],
            x.at[chip, :, at],
            cross_send.at[unit, r // CORES, k],
            cross_recv.at[unit, chip, k],
            samp=jnp.int32(r),
        )

    def cross_in(unit, r, g, k, at, sums, x):
        return remote(
            sums.at[g, :, at],
            x.at[g, :, at],
            cross_send.at[unit, g, k],
            cross_recv.at[unit, g, k],
            samp=sibling,
        )

    def owners(spans):
        return [(r, k, at) for r in range(peers) for k, at in enumerate(spans(r))]

    def send_pairs(unit, spans, p, q):
        for r, k, at in owners(spans):

            @pl.when(core != r % CORES)
            def _(r=r, k=k, at=at):
                pair(unit, r, k, at, p, q).start()

    def send_sums(unit, spans, p, q, sums, x):
        for r, k, at in owners(spans):

            @pl.when(core == r % CORES)
            def _(r=r, k=k, at=at):
                pair(unit, r, k, at, p, q).wait_recv()
                sums[r // CORES, :, at] = p[r % CORES, r // CORES, :, at] + q[r // CORES, :, at]

                @pl.when(chip != r // CORES)
                def _():
                    cross(unit, r, k, at, sums, x).start()

    def take_sums(unit, spans, sums, x, finish):
        for r, k, at in owners(spans):

            @pl.when(s == r)
            def _(r=r, k=k, at=at):
                value = sums[r // CORES, :, at]
                for g in range(chips):
                    if g != r // CORES:
                        cross_in(unit, r, g, k, at, sums, x).wait_recv()
                        value = value + x[g, :, at]
                finish(r, k, at, value)

    def wait_sends(unit, spans, p, q, sums, x):
        for r, k, at in owners(spans):

            @pl.when(core != r % CORES)
            def _(r=r, k=k, at=at):
                pair(unit, r, k, at, p, q).wait_send()

            @pl.when(jnp.logical_and(core == r % CORES, chip != r // CORES))
            def _(r=r, k=k, at=at):
                cross(unit, r, k, at, sums, x).wait_send()

    whole = pl.ds(0, width)

    def store_at(band, offset):
        def finish(r, k, at, value):
            out[band, :, pl.ds(at.start + offset, at.size)] = value * scales[band][:, : at.size]

        return finish

    for c in range(chunks):
        standardize(own, own_w, moments, c, own_t)
    for c in range(chunks):
        put(p0, 0, dot(own_t[...], own[c]), lanes(c))
    send_pairs(0, lambda r: [whole], p0, q0)
    send_sums(0, lambda r: [whole], p0, q0, s0, x0)

    @pl.when(has_upper)
    def _():
        moments_down().wait_recv()

    @pl.when(has_far)
    def _():
        moments_up().wait_recv()

    strip = pl.ds(0, LANES)

    def far_spans(c):
        def spans(r):
            q = r * rows // LANES
            if q < c:
                return [lanes(c)]
            if q == c < chunks - 1:
                return [pl.ds(0, (c + 1) * LANES)]
            if q == c:
                return [lanes(j) for j in range(chunks)]
            return []

        return spans

    def ship(c, k, at):
        return remote(
            far_out.at[:, at], far_in.at[:, at], far_send.at[c, k], far_recv.at[c, k], var=below
        )

    def take_chunk(c):
        @pl.when(has_far)
        def _():
            def finish(r, k, at, value):
                far_out[:, at] = value * scales[2][:, : at.size]
                ship(c, k, at).start()

            take_sums(1 + chunks + c, far_spans(c), s2, x2, finish)

        @pl.when(has_upper)
        def _():
            take_sums(1 + c, lambda r: [strip], s1.at[c], x1.at[c], store_at(1, c * LANES))

    for c in range(chunks):
        near, far = 1 + c, 1 + chunks + c
        near_refs = (p1.at[c], q1.at[c], s1.at[c], x1.at[c])
        far_refs = (p2, q2, s2, x2)

        for i, (first, size) in enumerate(pieces_of(samples, chunks, c)):
            at, add = pl.ds(first, size), i > 0

            @pl.when(has_upper)
            def _(c=c, i=i, first=first, size=size):
                down(c, i).wait_recv()
                standardize(upper, upper_w, upper_moments, c, None, (first, size))

            @pl.when(has_far)
            def _(c=c, i=i, at=at, add=add, first=first, size=size):
                up(c, i).wait_recv()
                standardize(lower, lower_w, lower_moments, c, lower_t, (first, size))
                for j in range(c + 1):
                    put(p2, c * LANES, dot(lower_t[lanes(c), at], upper[j, at, :]), lanes(j), add)
                if c:
                    put(p2, 0, dot(lower_t[: c * LANES, at], upper[c, at, :]), lanes(c), add)

            if first + size == samples:

                @pl.when(has_far)
                def _(c=c, far=far):
                    send_pairs(far, far_spans(c), p2, q2)

            @pl.when(has_upper)
            def _(c=c, at=at, add=add):
                put(p1.at[c], 0, dot(own_t[:, at], upper[c, at, :]), strip, add)

        @pl.when(has_upper)
        def _(c=c, near=near):
            send_pairs(near, lambda r: [strip], p1.at[c], q1.at[c])

        @pl.when(has_far)
        def _(c=c, far=far):
            send_sums(far, far_spans(c), *far_refs)

        @pl.when(has_upper)
        def _(c=c, near=near, near_refs=near_refs):
            send_sums(near, lambda r: [strip], *near_refs)

        if c == 0:
            take_sums(0, lambda r: [whole], s0, x0, store_at(0, 0))
        else:
            take_chunk(c - 1)

    take_chunk(chunks - 1)

    @pl.when(jnp.logical_not(has_upper))
    def _():
        out[1] = jnp.zeros((rows, width), jnp.float32)

    for c in range(chunks):
        for r, k, at in owners(far_spans(c)):

            @pl.when(jnp.logical_and(sends_up, s == r))
            def _(c=c, k=k, at=at):
                ship(c, k, at).wait_recv()

    @pl.when(sends_up)
    def _():
        out[2] = far_in[...]

    @pl.when(jnp.logical_not(sends_up))
    def _():
        out[2] = jnp.zeros((rows, width), jnp.float32)

    for o in range(1, peers):
        stat(o).wait_send()

    @pl.when(sends_down)
    def _():
        flags_down().wait_send()
        moments_down().wait_send()
        for item in bulk(down, range(chunks)):
            item().wait_send()

    @pl.when(sends_up)
    def _():
        flags_up().wait_send()
        moments_up().wait_send()
        for item in bulk(up, range(chunks)):
            item().wait_send()

    wait_sends(0, lambda r: [whole], p0, q0, s0, x0)

    @pl.when(has_upper)
    def _():
        for c in range(chunks):
            wait_sends(1 + c, lambda r: [strip], p1.at[c], q1.at[c], s1.at[c], x1.at[c])

    @pl.when(has_far)
    def _():
        for c in range(chunks):
            wait_sends(1 + chunks + c, far_spans(c), p2, q2, s2, x2)
            for r, k, at in owners(far_spans(c)):

                @pl.when(s == r)
                def _(c=c, k=k, at=at):
                    ship(c, k, at).wait_send()


def per_device(peers, depth, dosage, observed, band_reach):
    samples, width = dosage.shape
    chunks = width // LANES
    rows = width // peers
    chips = peers // CORES
    half, full = jnp.bfloat16, jnp.float32
    dma = pltpu.SemaphoreType.DMA
    units = 1 + 2 * chunks
    block = pltpu.VMEM((chunks, samples, LANES), half)
    turned = pltpu.VMEM((width, samples), half)
    column = pltpu.VMEM((samples, LANES), full)
    flags = pltpu.VMEM((1, samples), jnp.int32)
    terms = pltpu.VMEM((8, width), full)
    wide = [pltpu.VMEM((CORES, chips, rows, width), full)] + [
        pltpu.VMEM((chips, rows, width), full)
    ] * 3
    strips = [pltpu.VMEM((chunks, CORES, chips, rows, LANES), full)] + [
        pltpu.VMEM((chunks, chips, rows, LANES), full)
    ] * 3
    result = pltpu.VMEM((rows, width), full)
    values = pl.pallas_call(
        functools.partial(band_kernel, peers, depth),
        out_shape=jax.ShapeDtypeStruct((BAND, rows, width), full),
        in_specs=[pl.BlockSpec(memory_space=pl.ANY)] * 2,
        out_specs=pl.BlockSpec(memory_space=pltpu.VMEM),
        scratch_shapes=[block] * 3
        + [turned] * 2
        + [column] * 3
        + [flags] * 3
        + [pltpu.VMEM((peers, 8, width), full)]
        + [terms] * 3
        + wide
        + strips
        + wide
        + [result] * 2
        + [dma((chunks + 1,)), dma((peers,)), dma((peers,)), dma((4,)), dma((4,))]
        + [dma((sum(len(pieces_of(samples, chunks, c)) for c in range(chunks)),))] * 4
        + [dma((units, chips, chunks))] * 4
        + [dma((chunks, chunks))] * 2,
        compiler_params=pltpu.CompilerParams(
            collective_id=0, has_side_effects=True, vmem_limit_bytes=52 * 1024 * 1024
        ),
        cost_estimate=pl.CostEstimate(
            flops=2 * BAND * width * width * samples,
            bytes_accessed=2 * samples * width,
            transcendentals=0,
        ),
    )(dosage, observed)
    keep = jnp.arange(BAND, dtype=jnp.int32) <= band_reach[0]
    return jnp.where(
        keep[None, None, :, None], jnp.transpose(values, (1, 0, 2))[None], jnp.float32(0.0)
    )


def solution(mesh):
    return jax.shard_map(
        functools.partial(per_device, mesh.shape["samp"], mesh.shape["var"]),
        mesh=mesh,
        in_specs=(P("samp", ("seg", "var")), P(("seg", "var"), "samp"), P(("seg", "var"))),
        out_specs=P(("seg", "var"), "samp", None, None),
        check_vma=False,
    )
```
